32 devices in a mesh: leaf: 8 (over y, x, core), grp: 4 (over z).
Axes of the slice: x: 2, y: 2, z: 4, core: 2. Of those that a mesh axis runs over, the one named last changes fastest.
Arguments:
- low_rhs: float32 [8192, 1024], P('leaf', 'grp'), may hold values from -6 to 6
- low_inverse: float32 [8192, 1024], P(('leaf', 'grp')), as said below
- panels: float32 [8192, 1024], P(('leaf', 'grp')), may hold values from -0.1875 to 0.1875
- row_blocks: int32 [8, 8], P('leaf'), may hold values from 0 to 15, all different within a row
- root_rhs: float32 [2048, 1024], P('leaf', 'grp'), may hold values from -6 to 6
- root_inverse: float32 [2048, 2048], P('leaf'), as said below
Outputs:
- low_solution: float32 [8192, 1024], P('leaf', 'grp')
- root_solution: float32 [2048, 1024], P('leaf', 'grp')
The draws below stay inside these ranges and needn't reach their ends.
Inputs may be any that keep to these rules, and one draw needn't show every extreme that they name: `row_blocks`: each row names 8 different root blocks, and every root block is named by some row. `low_inverse`: lower triangular, with a positive diagonal. `root_inverse`: lower triangular, with a positive diagonal.
All inputs are finite; a program needn't handle non-finite values.
Results may differ from the reference program's by a relative error of at most 0.0003.
Values sent between devices are 32-bit elements; how exact they have to be, the bound alone decides.
A program may use at most 64 MiB of HBM per device.

```python
import jax
import jax.numpy as jnp
from jax import lax

W = 1024
BLK = 128
NB = 16
K = 8
NS = 8
WR = 2048
SAMPLES = 1024


def triangle(key, count, width):
    key_diag, key_off = jax.random.split(key)
    rows = jnp.arange(width)[:, None]
    cols = jnp.arange(width)[None, :]
    diag_vals = jnp.exp(jax.random.uniform(key_diag, (count, width, 1), jnp.float32, jnp.log(0.5), jnp.log(2.0)))
    off_vals = jax.random.normal(key_off, (count, width, width), jnp.float32)
    off_vals = off_vals * (0.6 / jnp.sqrt(width * 1.0))
    lower = jnp.where(cols < rows, off_vals, 0.0)
    return lower + jnp.where(cols == rows, diag_vals, 0.0)


def draw_low_inverse(key, part):
    return triangle(jax.random.fold_in(key, 11), NS, W).reshape(NS * W, W)


def draw_root_inverse(key, part):
    return triangle(jax.random.fold_in(key, 23), 1, WR).reshape(WR, WR)


def levels(own_key, dims, cuts, least, top_value):
    gain, own = 1.0, jax.random.fold_in(own_key, 6)
    for dim, shards_of in cuts:
        draws = jnp.exp(jax.random.uniform(jax.random.fold_in(own, dim), (shards_of,), jnp.float32, least / len(cuts), top_value / len(cuts)))
        gain = gain * jnp.repeat(draws, dims[dim] // shards_of).reshape([-1 if axis == dim else 1 for axis in range(len(dims))])
    return gain


def distinct(own_key, rows, number_of, top, lift):
    ranking = jax.random.permutation(jax.random.fold_in(own_key, 1), number_of)
    boost = ranking
    for power in range(3):
        boost = boost * boost // number_of
    boost = boost * lift // number_of
    lots = jax.random.randint(jax.random.fold_in(own_key, 2), (rows, number_of), 0, 4096) + boost
    sure = jax.random.permutation(jax.random.fold_in(own_key, 3), rows)[jnp.arange(number_of) % rows]
    lots = jnp.where(jnp.arange(rows)[:, None] == sure[None, :], 1 << 14, lots)
    score = lots * number_of + jnp.arange(number_of)
    return lax.top_k(score.astype(jnp.int32), top)[1].astype(jnp.int32)


def normal_values(stream_key, extent, deviation, most, cuts=(), dtype=jnp.bfloat16):
    drawn = deviation * jax.random.normal(stream_key, extent, jnp.float32)
    if cuts:
        drawn = drawn * levels(stream_key, extent, cuts, -0.22, 0.18)
    return jnp.clip(drawn, -most, most).astype(dtype)


def setup_inputs(seed: int = 0) -> dict:
    key_of = jax.random.split(jax.random.key(seed), 7)
    low_rhs = normal_values(key_of[0], (NS * W, SAMPLES), 1.0, 6.0, ((0, 8), (1, 4)), jnp.float32)
    low_inverse = draw_low_inverse(jax.random.fold_in(key_of[6], 71), 0)
    panels = normal_values(key_of[2], (NS * K * BLK, W), W ** -0.5, 0.1875, ((0, 32),), jnp.float32)
    row_blocks = distinct(key_of[3], NS, NB, K, 0)
    root_rhs = normal_values(key_of[4], (WR, SAMPLES), 1.0, 6.0, ((0, 8), (1, 4)), jnp.float32)
    root_inverse = draw_root_inverse(jax.random.fold_in(key_of[6], 71), 0)
    return dict(low_rhs=low_rhs, low_inverse=low_inverse, panels=panels, row_blocks=row_blocks, root_rhs=root_rhs, root_inverse=root_inverse)


def reference(low_rhs, low_inverse, panels, row_blocks, root_rhs, root_inverse):
    inverses = low_inverse.reshape(NS, W, W)
    rights = low_rhs.reshape(NS, W, SAMPLES)
    panel_set = panels.reshape(NS, K * BLK, W)

    def one_node(total, items):
        inverse_s, right_s, panel_s, blocks_s = items
        solved = jnp.dot(inverse_s, right_s, precision=lax.Precision.HIGHEST)
        update = jnp.dot(panel_s, solved, precision=lax.Precision.HIGHEST).reshape(K, BLK, SAMPLES)
        total = total.at[blocks_s.astype(jnp.int32)].add(update)
        return total, solved

    start = jnp.zeros((NB, BLK, SAMPLES), jnp.float32)
    total, solved_all = lax.scan(one_node, start, (inverses, rights, panel_set, row_blocks))
    combined = root_rhs - total.reshape(WR, SAMPLES)
    root_solution = jnp.dot(root_inverse, combined, precision=lax.Precision.HIGHEST)
    return solved_all.reshape(NS * W, SAMPLES), root_solution
```

```python
import functools

import jax
import jax.numpy as jnp
from jax import lax
from jax.experimental import pallas as pl
from jax.experimental.pallas import tpu as pltpu
from jax.sharding import PartitionSpec as P

MESH = pl.DeviceIdType.MESH
F32, BF16 = jnp.float32, jnp.bfloat16

LO, RO, PO = 0, 4, 8
LI, LF, PI, PF = 12, 16, 20, 24
XO, FO = 28, 32
CS, RA, RB, AG = 33, 37, 41, 43
COPIES = 53


def split(v):
    hi = v.astype(BF16)
    return hi, (v - hi.astype(F32)).astype(BF16)


def dot3(a, b):
    ah, al = a
    bh, bl = b
    d = functools.partial(jnp.dot, preferred_element_type=F32)
    return d(ah, bh) + (d(ah, bl) + d(al, bh))


def kernel(inv, low_rhs, low_inverse, panels, root_rhs, root_inverse,
           low_out, root_out,
           lbuf, pbuf, rbuf, xbuf, xh, xl, ubuf, sbuf, cbuf, tbuf, ra, rb, fs, rz,
           gbuf, ribuf, rih, ril, ss, rs, ls):
    leaf, grp = lax.axis_index("leaf"), lax.axis_index("grp")
    planes = lax.axis_size("grp")
    width, cols = low_rhs.shape
    q_rows = low_inverse.shape[0]
    own_rows = root_rhs.shape[0]
    blk = own_rows // 2
    pc = q_rows // 4
    y, x, c = leaf // 4, (leaf // 2) % 2, leaf % 2
    inner = jnp.logical_and(grp > 0, grp < planes - 1)
    outer = jnp.logical_not(inner)
    low_side = grp < 2
    mate = jnp.where(low_side, 1 - grp, 5 - grp)
    other = 3 - grp
    side_q = jnp.where(low_side, 0, planes - 1)
    z_mate, z_other = (leaf, mate), (leaf, other)
    x_dev = (leaf + 2 - 4 * x, grp)
    y_dev = (leaf + 4 - 8 * y, grp)
    c_dev = (leaf + 1 - 2 * c, grp)

    def rc(n, src, dst, dev):
        return pltpu.make_async_remote_copy(
            src_ref=src, dst_ref=dst, send_sem=ss.at[n], recv_sem=rs.at[n],
            device_id=dev, device_id_type=MESH)

    def rows(start, n):
        return pl.ds(pl.multiple_of(start, n), n)

    def l_slot(q, k):
        return lbuf.at[rows(q * q_rows, q_rows), pl.ds(k * q_rows, q_rows)]

    def p_slot(q, k):
        return pbuf.at[rows(q * q_rows + k * pc, pc)]

    def l_in(k):
        return low_inverse.at[:, pl.ds(k * q_rows, q_rows)]

    def when(cond):
        return pl.when(cond)

    barrier = pltpu.get_barrier_semaphore()
    for dev in (x_dev, y_dev, c_dev, z_mate):
        pl.semaphore_signal(barrier, inc=1, device_id=dev, device_id_type=MESH)

    @when(inner)
    def _():
        pl.semaphore_signal(barrier, inc=1, device_id=z_other, device_id_type=MESH)

    ri_copy = pltpu.make_async_copy(root_inverse, ribuf, ls.at[0])
    ri_copy.start()
    x_own = pltpu.make_async_copy(xbuf.at[1], low_out, ls.at[4])
    l_own = pltpu.make_async_copy(low_inverse, lbuf.at[rows(grp * q_rows, q_rows)], ls.at[1])
    p_own = pltpu.make_async_copy(panels, pbuf.at[rows(grp * q_rows, q_rows)], ls.at[2])
    r_own = pltpu.make_async_copy(low_rhs, rbuf.at[1], ls.at[3])

    @when(inner)
    def _():
        l_own.start()
        r_own.start()
        p_own.start()
        pl.semaphore_wait(barrier, 5)

    @when(outer)
    def _():
        pl.semaphore_wait(barrier, 4)

    quarter = width // 4

    def lo(k):
        return rc(LO + k, l_in(k), l_slot(side_q, k), z_mate)

    def ro(k):
        part = pl.ds(k * quarter, quarter)
        return rc(RO + k, low_rhs.at[part], rbuf.at[0, part], z_mate)

    def po(k):
        return rc(PO + k, panels.at[pl.ds(k * pc, pc)], p_slot(side_q, k), z_mate)

    def xo(k):
        part = pl.ds(k * quarter, quarter)
        return rc(XO + k, xbuf.at[0, part], low_out.at[part], z_mate)

    f_out = rc(FO, fs, rz, z_mate)

    def split_ri():
        ri_copy.wait()
        for j in range(root_inverse.shape[1] // own_rows):
            hi, lo_part = split(ribuf[:, j * own_rows:(j + 1) * own_rows])
            rih[j] = hi
            ril[j] = lo_part

    @when(outer)
    def _():
        todo = [(k, lo(k)) for k in range(4)]
        todo += [(0, ro(k)) for k in range(4)] + [(0, po(k)) for k in range(4)]
        for n, (need, copy) in enumerate(todo):
            if n >= 3:
                before, earlier = todo[n - 3]

                @when(before <= grp)
                def _():
                    earlier.wait_send()

            @when(need <= grp)
            def _():
                copy.start()
        split_ri()
        for need, copy in todo[-3:]:
            copy.wait_send()
        for k in range(4):
            xo(k).wait_recv()
        f_out.wait_recv()
        gbuf[0, 0] = root_rhs[...] - rz[...]

    @when(inner)
    def _():
        def li(k, q):
            return rc(LI + k, l_in(k), l_slot(q, k), z_other)

        def lf(k, q):
            return rc(LF + k, l_slot(q, k), l_slot(q, k), z_other)

        def pi(k, q):
            return rc(PI + k, panels.at[pl.ds(k * pc, pc)], p_slot(q, k), z_other)

        def pf(k, q):
            return rc(PF + k, p_slot(q, k), p_slot(q, k), z_other)

        far = planes - 1 - side_q
        for k in range(4):
            @when(k <= grp)
            def _():
                li(k, grp).start()
        split_ri()
        for k in range(4):
            @when(k <= side_q)
            def _():
                lo(k).wait_recv()
                lf(k, side_q).start()
        for k in range(4):
            @when(k <= grp)
            def _():
                li(k, grp).wait_send()
        for k in range(4):
            pi(k, grp).start()

        l_own.wait()
        r_own.wait()
        for k in range(4):
            ro(k).wait_recv()
        for k in range(4):
            @when(k <= other)
            def _():
                li(k, other).wait_recv()

            @when(k <= far)
            def _():
                lf(k, far).wait_recv()
        for h in range(2):
            r_all = split(rbuf[h])
            for r in range(4):
                depth = (r + 1) * quarter
                here = slice(r * quarter, (r + 1) * quarter)
                part = dot3(split(lbuf[here, :depth]), (r_all[0][:depth], r_all[1][:depth]))
                xbuf[h, here] = part
                hi, lo_part = split(part)
                xh[here, h * cols:(h + 1) * cols] = hi
                xl[here, h * cols:(h + 1) * cols] = lo_part
                if h == 0:
                    xo(r).start()
        x_own.start()

        def update(q):
            at = rows(q * q_rows, q_rows)
            part = dot3(split(pbuf[at, :]), (xh[...], xl[...]))
            per = q_rows // blk
            for n in range(per):
                ubuf[q * per + n] = part[n * blk:(n + 1) * blk]

        ubuf[width // blk] = jnp.zeros((blk, 2 * cols), F32)
        p_own.wait()
        update(grp)
        for k in range(4):
            po(k).wait_recv()
            pf(k, side_q).start()
        update(side_q)
        for k in range(4):
            pi(k, other).wait_recv()
        update(other)
        for k in range(4):
            pf(k, far).wait_recv()
        update(far)

        def named(d, core, j):
            dy, dx = d // 2, d % 2
            yy, xx = y + dy - 2 * dy * y, x + dx - 2 * dx * x
            r = ((yy * 2 + xx) * 2 + core) * 2 + j
            return ubuf[inv[0, r]]

        order = (3, 1, 2, 0)
        cs = [rc(CS + d, sbuf.at[d], cbuf.at[d], c_dev) for d in range(4)]
        for d in order:
            for j in range(2):
                u = named(d, 1 - c, j)
                for h in range(2):
                    sbuf[d, h, j * blk:(j + 1) * blk] = u[:, h * cols:(h + 1) * cols]
            cs[d].start()
        a0 = [rc(RA, tbuf.at[1, 0], ra.at[0], x_dev), rc(RA + 1, tbuf.at[3, 0], ra.at[1], x_dev)]
        a1 = [rc(RA + 2, tbuf.at[2, 1], ra.at[2], y_dev), rc(RA + 3, tbuf.at[3, 1], ra.at[3], y_dev)]
        b0 = rc(RB, tbuf.at[2, 0], rb.at[0], y_dev)
        b1 = rc(RB + 1, tbuf.at[1, 1], rb.at[1], x_dev)
        for d in order:
            cs[d].wait_recv()
            for j in range(2):
                u = named(d, c, j)
                here = slice(j * blk, (j + 1) * blk)
                for h in range(2):
                    tbuf[d, h, here] = u[:, h * cols:(h + 1) * cols] + cbuf[d, h, here]
            if d == 3:
                a0[1].start()
                a1[1].start()
            elif d == 1:
                a0[0].start()
            elif d == 2:
                a1[0].start()
        a0[1].wait_recv()
        tbuf[2, 0] += ra[1]
        b0.start()
        a1[1].wait_recv()
        tbuf[1, 1] += ra[3]
        b1.start()
        a0[0].wait_recv()
        b0.wait_recv()
        fs[...] = tbuf[0, 0] + ra[0] + rb[0]
        f_out.start()
        a1[0].wait_recv()
        b1.wait_recv()
        gbuf[0, 0] = root_rhs[...] - (tbuf[0, 1] + ra[2] + rb[1])
        for k in range(4):
            @when(k <= side_q)
            def _():
                lf(k, side_q).wait_send()
            pi(k, grp).wait_send()
            pf(k, side_q).wait_send()
            xo(k).wait_send()
            cs[k].wait_send()
        for copy in a0 + a1 + [b0, b1, f_out]:
            copy.wait_send()
        x_own.wait()

    half = [pl.ds(0, blk), pl.ds(blk, blk)]

    def g_half(d, h):
        return gbuf.at[d, 0, half[h]]

    ag = [
        rc(AG, g_half(0, 0), g_half(1, 0), x_dev),
        rc(AG + 1, g_half(0, 1), g_half(2, 1), y_dev),
        rc(AG + 2, g_half(0, 0), g_half(2, 0), y_dev),
        rc(AG + 3, g_half(0, 1), g_half(1, 1), x_dev),
        rc(AG + 4, gbuf.at[0, 0], gbuf.at[0, 1], c_dev),
        rc(AG + 5, g_half(1, 0), g_half(3, 0), y_dev),
        rc(AG + 6, g_half(2, 1), g_half(3, 1), x_dev),
        rc(AG + 7, gbuf.at[1, 0], gbuf.at[1, 1], c_dev),
        rc(AG + 8, gbuf.at[2, 0], gbuf.at[2, 1], c_dev),
        rc(AG + 9, gbuf.at[3, 0], gbuf.at[3, 1], c_dev),
    ]

    def term(d, dc):
        dy, dx = d // 2, d % 2
        yy, xx = y + dy - 2 * dy * y, x + dx - 2 * dx * x
        j = (yy * 2 + xx) * 2 + (c if dc == 0 else 1 - c)
        return dot3((rih[j], ril[j]), split(gbuf[d, dc]))

    for n in (0, 1, 4, 2, 3):
        ag[n].start()
    root_out[...] = term(0, 0)
    ag[0].wait_recv()
    ag[5].start()
    ag[1].wait_recv()
    ag[6].start()
    ag[4].wait_recv()
    root_out[...] += term(0, 1)
    ag[3].wait_recv()
    ag[7].start()
    ag[2].wait_recv()
    ag[8].start()
    root_out[...] += term(1, 0) + term(2, 0)
    ag[7].wait_recv()
    ag[8].wait_recv()
    root_out[...] += term(1, 1) + term(2, 1)
    ag[5].wait_recv()
    ag[6].wait_recv()
    ag[9].start()
    root_out[...] += term(3, 0)
    ag[9].wait_recv()
    root_out[...] += term(3, 1)
    for copy in ag:
        copy.wait_send()


def fused(low_rhs, low_inverse, panels, row_blocks, root_rhs, root_inverse):
    width, cols = low_rhs.shape
    own_rows, root = root_inverse.shape
    k_blocks = row_blocks.shape[1]
    blk = width // k_blocks
    hit = row_blocks[0][None, :] == jnp.arange(root // blk, dtype=jnp.int32)[:, None]
    names = jnp.arange(k_blocks, dtype=jnp.int32)
    inv = jnp.min(jnp.where(hit, names[None, :], k_blocks), axis=1).astype(jnp.int32)[None]
    vm = pltpu.VMEM
    any_spec = pl.BlockSpec(memory_space=pl.ANY)
    vm_spec = pl.BlockSpec(memory_space=vm)
    block = (own_rows, cols)
    return pl.pallas_call(
        kernel,
        out_shape=(jax.ShapeDtypeStruct(low_rhs.shape, F32), jax.ShapeDtypeStruct(root_rhs.shape, F32)),
        in_specs=[pl.BlockSpec(memory_space=pltpu.SMEM), any_spec, any_spec, any_spec, vm_spec, any_spec],
        out_specs=(any_spec, vm_spec),
        scratch_shapes=[
            vm((width, width), F32),
            vm((width, width), F32),
            vm((2, width, cols), F32),
            vm((2, width, cols), F32),
            vm((width, 2 * cols), BF16),
            vm((width, 2 * cols), BF16),
            vm((k_blocks + 1, blk, 2 * cols), F32),
            vm((4, 2) + block, F32),
            vm((4, 2) + block, F32),
            vm((4, 2) + block, F32),
            vm((4,) + block, F32),
            vm((2,) + block, F32),
            vm(block, F32),
            vm(block, F32),
            vm((4, 2) + block, F32),
            vm((own_rows, root), F32),
            vm((root // own_rows, own_rows, own_rows), BF16),
            vm((root // own_rows, own_rows, own_rows), BF16),
            pltpu.SemaphoreType.DMA((COPIES,)),
            pltpu.SemaphoreType.DMA((COPIES,)),
            pltpu.SemaphoreType.DMA((5,)),
        ],
        compiler_params=pltpu.CompilerParams(
            collective_id=0, has_side_effects=True, vmem_limit_bytes=56 * 2**20),
        cost_estimate=pl.CostEstimate(flops=2 * 10**10, bytes_accessed=10**7, transcendentals=0),
    )(inv, low_rhs, low_inverse, panels, root_rhs, root_inverse)


def general(low_rhs, low_inverse, panels, row_blocks, root_rhs, root_inverse):
    cols = low_rhs.shape[1]
    k_blocks = row_blocks.shape[1]
    root = root_inverse.shape[1]
    blk = low_rhs.shape[0] // k_blocks
    high = lax.Precision.HIGHEST
    low_solution = jnp.dot(lax.all_gather(low_inverse, "grp", axis=0, tiled=True), low_rhs, precision=high)
    update = jnp.dot(lax.all_gather(panels, "grp", axis=0, tiled=True), low_solution, precision=high)
    onehot = (row_blocks[0][None, :] == jnp.arange(root // blk, dtype=jnp.int32)[:, None]).astype(F32)
    placed = jnp.dot(onehot, update.reshape(k_blocks, blk * cols), precision=high).reshape(root, cols)
    arrived = lax.all_to_all(placed, "leaf", split_axis=0, concat_axis=0, tiled=True)
    gathered = jnp.sum(arrived.reshape((-1,) + root_rhs.shape), axis=0)
    combined = lax.all_gather(root_rhs - gathered, "leaf", axis=0, tiled=True)
    return low_solution, jnp.dot(root_inverse, combined, precision=high)


def solution(mesh):
    placed = (
        P("leaf", "grp"),
        P(("leaf", "grp"), None),
        P(("leaf", "grp"), None),
        P("leaf", None),
        P("leaf", "grp"),
        P("leaf", None),
    )
    body = fused if (mesh.shape["leaf"], mesh.shape["grp"]) == (8, 4) else general
    return jax.shard_map(
        body,
        mesh=mesh,
        in_specs=placed,
        out_specs=(P("leaf", "grp"), P("leaf", "grp")),
        check_vma=False,
    )
```

```python
import functools

import jax
import jax.numpy as jnp
from jax import lax
from jax.experimental import pallas as pl
from jax.experimental.pallas import tpu as pltpu
from jax.sharding import PartitionSpec as P

MESH = pl.DeviceIdType.MESH
F32, BF16 = jnp.float32, jnp.bfloat16

LO, RO, PO = 0, 5, 9
LI, LF, PI, PF = 13, 18, 23, 27
XO, FO = 31, 35
CS, RA, RB, AG = 37, 45, 53, 57
COPIES = 67


def split(v):
    hi = v.astype(BF16)
    return hi, (v - hi.astype(F32)).astype(BF16)


def dot3(a, b):
    ah, al = a
    bh, bl = b
    d = functools.partial(jnp.dot, preferred_element_type=F32)
    return d(ah, bh) + (d(ah, bl) + d(al, bh))


def kernel(names, low_rhs, low_inverse, panels, root_rhs, root_inverse,
           low_out, root_out,
           lbuf, pbuf, rbuf, xbuf, xh, xl, ubuf, sbuf, cbuf, tbuf, ra, rb, fs, rz,
           gbuf, ribuf, rih, ril, ss, rs, ls):
    leaf, grp = lax.axis_index("leaf"), lax.axis_index("grp")
    planes = lax.axis_size("grp")
    width, cols = low_rhs.shape
    q_rows = low_inverse.shape[0]
    own_rows = root_rhs.shape[0]
    blk = own_rows // 2
    pc = q_rows // 4
    y, x, c = leaf // 4, (leaf // 2) % 2, leaf % 2
    inner = jnp.logical_and(grp > 0, grp < planes - 1)
    outer = jnp.logical_not(inner)
    low_side = grp < 2
    mate = jnp.where(low_side, 1 - grp, 5 - grp)
    other = 3 - grp
    side_q = jnp.where(low_side, 0, planes - 1)
    z_mate, z_other = (leaf, mate), (leaf, other)
    x_dev = (leaf + 2 - 4 * x, grp)
    y_dev = (leaf + 4 - 8 * y, grp)
    c_dev = (leaf + 1 - 2 * c, grp)

    def rc(n, src, dst, dev):
        return pltpu.make_async_remote_copy(
            src_ref=src, dst_ref=dst, send_sem=ss.at[n], recv_sem=rs.at[n],
            device_id=dev, device_id_type=MESH)

    def rows(start, n):
        return pl.ds(pl.multiple_of(start, n), n)

    edge = q_rows // 2

    def l_part(q, k):
        if k < 3:
            return 0, q_rows, pl.ds(k * q_rows, q_rows)
        if k == 3:
            return 0, q_rows, pl.ds(pl.multiple_of(q * q_rows, q_rows), edge)
        return edge, edge, pl.ds(pl.multiple_of(q * q_rows + edge, edge), edge)

    def l_need(k):
        return k + 1 if k < 3 else 0

    def l_slot(q, k):
        first, count, at = l_part(q, k)
        return lbuf.at[rows(q * q_rows + first, count), at]

    def p_slot(q, k):
        return pbuf.at[rows(q * q_rows + k * pc, pc)]

    def l_in(q, k):
        first, count, at = l_part(q, k)
        return low_inverse.at[pl.ds(first, count), at]

    def when(cond):
        return pl.when(cond)

    barrier = pltpu.get_barrier_semaphore()
    for dev in (x_dev, y_dev, c_dev, z_mate):
        pl.semaphore_signal(barrier, inc=1, device_id=dev, device_id_type=MESH)

    @when(inner)
    def _():
        pl.semaphore_signal(barrier, inc=1, device_id=z_other, device_id_type=MESH)

    ri_copy = pltpu.make_async_copy(root_inverse, ribuf, ls.at[0])
    ri_copy.start()
    x_own = pltpu.make_async_copy(xbuf.at[1], low_out, ls.at[4])
    l_own = pltpu.make_async_copy(low_inverse, lbuf.at[rows(grp * q_rows, q_rows)], ls.at[1])
    p_own = pltpu.make_async_copy(panels, pbuf.at[rows(grp * q_rows, q_rows)], ls.at[2])
    r_own = pltpu.make_async_copy(low_rhs, rbuf.at[1], ls.at[3])

    @when(inner)
    def _():
        l_own.start()
        r_own.start()
        p_own.start()
        pl.semaphore_wait(barrier, 5)

    @when(outer)
    def _():
        pl.semaphore_wait(barrier, 4)

    quarter = width // 4

    def lo(k):
        return rc(LO + k, l_in(side_q, k), l_slot(side_q, k), z_mate)

    def ro(k):
        part = pl.ds(k * quarter, quarter)
        return rc(RO + k, low_rhs.at[part], rbuf.at[0, part], z_mate)

    def po(k):
        return rc(PO + k, panels.at[pl.ds(k * pc, pc)], p_slot(side_q, k), z_mate)

    def xo(k):
        part = pl.ds(k * quarter, quarter)
        return rc(XO + k, xbuf.at[0, part], low_out.at[part], z_mate)

    half = [pl.ds(0, blk), pl.ds(blk, blk)]
    f_out = [rc(FO + k, fs.at[half[k]], rz.at[half[k]], z_mate) for k in range(2)]

    def split_ri():
        ri_copy.wait()
        for j in range(root_inverse.shape[1] // own_rows):
            hi, lo_part = split(ribuf[:, j * own_rows:(j + 1) * own_rows])
            rih[j] = hi
            ril[j] = lo_part

    @when(outer)
    def _():
        todo = [(l_need(k), lo(k)) for k in range(5)]
        todo += [(0, ro(k)) for k in range(4)] + [(0, po(k)) for k in range(4)]
        for n, (need, copy) in enumerate(todo):
            if n >= 3:
                before, earlier = todo[n - 3]

                @when(before <= grp)
                def _():
                    earlier.wait_send()

            @when(need <= grp)
            def _():
                copy.start()
        split_ri()
        for need, copy in todo[-3:]:
            copy.wait_send()
        for k in range(4):
            xo(k).wait_recv()
        for k in range(2):
            f_out[k].wait_recv()
            gbuf[0, 0, half[k]] = root_rhs[half[k], :] - rz[half[k], :]

    @when(inner)
    def _():
        def li(k, q):
            return rc(LI + k, l_in(grp, k), l_slot(q, k), z_other)

        def lf(k, q):
            return rc(LF + k, l_slot(q, k), l_slot(q, k), z_other)

        def pi(k, q):
            return rc(PI + k, panels.at[pl.ds(k * pc, pc)], p_slot(q, k), z_other)

        def pf(k, q):
            return rc(PF + k, p_slot(q, k), p_slot(q, k), z_other)

        far = planes - 1 - side_q
        for k in range(5):
            @when(l_need(k) <= grp)
            def _():
                li(k, grp).start()
        pi(0, grp).start()
        split_ri()
        for q in (side_q, other, far):
            lbuf[rows(q * q_rows, edge), pl.ds(pl.multiple_of(q * q_rows + edge, edge), edge)] = (
                jnp.zeros((edge, edge), F32))
        pi(1, grp).start()
        for k in range(5):
            @when(l_need(k) <= side_q)
            def _():
                lo(k).wait_recv()
                lf(k, side_q).start()
        for k in range(5):
            @when(l_need(k) <= grp)
            def _():
                li(k, grp).wait_send()
        for k in range(2, 4):
            pi(k, grp).start()

        l_own.wait()
        r_own.wait()
        for k in range(4):
            ro(k).wait_recv()
        for k in range(5):
            @when(l_need(k) <= other)
            def _():
                li(k, other).wait_recv()

            @when(l_need(k) <= far)
            def _():
                lf(k, far).wait_recv()
        for h in range(2):
            r_all = split(rbuf[h])
            for r in range(4):
                depth = (r + 1) * quarter
                here = slice(r * quarter, (r + 1) * quarter)
                part = dot3(split(lbuf[here, :depth]), (r_all[0][:depth], r_all[1][:depth]))
                xbuf[h, here] = part
                hi, lo_part = split(part)
                xh[here, h * cols:(h + 1) * cols] = hi
                xl[here, h * cols:(h + 1) * cols] = lo_part
                if h == 0:
                    xo(r).start()
        x_own.start()

        slots = width // blk + 1

        def update(first, count, hs=(0, 1)):
            panel = split(pbuf[rows(first * blk, count * blk), :])
            for h in hs:
                at = slice(h * cols, (h + 1) * cols)
                part = dot3(panel, (xh[:, at], xl[:, at]))
                for n in range(count):
                    ubuf[h * slots + first + n] = part[n * blk:(n + 1) * blk]

        per = q_rows // blk
        for h in range(2):
            ubuf[h * slots + slots - 1] = jnp.zeros((blk, cols), F32)
        p_own.wait()
        update(grp * per, per)
        for k in range(4):
            po(k).wait_recv()
            pf(k, side_q).start()
        update(side_q * per, per)
        for k in range(4):
            pi(k, other).wait_recv()
        update(other * per, per)

        def named(d, core, j, h):
            dy, dx = d // 2, d % 2
            yy, xx = y + dy - 2 * dy * y, x + dx - 2 * dx * x
            r = ((yy * 2 + xx) * 2 + core) * 2 + j
            at = jnp.int32(slots - 1)
            for k in range(slots - 1):
                at = jnp.where(names[0, k] == r, k, at)
            return ubuf[h * slots + at]

        order = (3, 1, 2, 0)
        top, low = half
        cs, steps, b0, b1 = [], [], [], []
        for h in range(2):
            cs.append([rc(CS + 4 * h + d, sbuf.at[d, h], cbuf.at[d, h], c_dev) for d in range(4)])
            steps.append([
                rc(RA + 4 * h, tbuf.at[1, h, top], ra.at[h, 0], x_dev),
                rc(RA + 4 * h + 1, tbuf.at[3, h, top], ra.at[h, 1], x_dev),
                rc(RA + 4 * h + 2, tbuf.at[2, h, low], ra.at[h, 2], y_dev),
                rc(RA + 4 * h + 3, tbuf.at[3, h, low], ra.at[h, 3], y_dev)])
            b0.append(rc(RB + 2 * h, tbuf.at[2, h, top], rb.at[h, 0], y_dev))
            b1.append(rc(RB + 2 * h + 1, tbuf.at[1, h, low], rb.at[h, 1], x_dev))

        def to_core(h):
            for d in order:
                for j in range(2):
                    sbuf[d, h, half[j]] = named(d, 1 - c, j, h)
                cs[h][d].start()

        def from_core(h):
            for d in order:
                cs[h][d].wait_recv()
                for j in range(2):
                    tbuf[d, h, half[j]] = named(d, c, j, h) + cbuf[d, h, half[j]]
                for n in {3: (1, 3), 1: (0,), 2: (2,), 0: ()}[d]:
                    steps[h][n].start()

        def second(h):
            steps[h][1].wait_recv()
            tbuf[2, h, top] += ra[h, 1]
            b0[h].start()
            steps[h][3].wait_recv()
            tbuf[1, h, low] += ra[h, 3]
            b1[h].start()

        def final(h, k):
            steps[h][2 * k].wait_recv()
            (b0, b1)[k][h].wait_recv()
            return tbuf[0, h, half[k]] + ra[h, 2 * k] + rb[h, k]

        for k in range(2):
            pf(k, far).wait_recv()
        update(far * per, 1)
        for k in range(2, 4):
            pf(k, far).wait_recv()
        update(far * per + 1, 1, (0,))
        to_core(0)
        update(far * per + 1, 1, (1,))
        to_core(1)
        from_core(0)
        second(0)
        from_core(1)
        for k in range(2):
            fs[half[k], :] = final(0, k)
            f_out[k].start()
        second(1)
        for k in range(2):
            gbuf[0, 0, half[k]] = root_rhs[half[k], :] - final(1, k)
        for k in range(5):
            @when(l_need(k) <= side_q)
            def _():
                lf(k, side_q).wait_send()
        for k in range(4):
            pi(k, grp).wait_send()
            pf(k, side_q).wait_send()
            xo(k).wait_send()
        for copy in cs[0] + cs[1] + steps[0] + steps[1] + b0 + b1 + f_out:
            copy.wait_send()
        x_own.wait()

    def g_half(d, h):
        return gbuf.at[d, 0, half[h]]

    ag = [
        rc(AG, g_half(0, 0), g_half(1, 0), x_dev),
        rc(AG + 1, g_half(0, 1), g_half(2, 1), y_dev),
        rc(AG + 2, g_half(0, 0), g_half(2, 0), y_dev),
        rc(AG + 3, g_half(0, 1), g_half(1, 1), x_dev),
        rc(AG + 4, gbuf.at[0, 0], gbuf.at[0, 1], c_dev),
        rc(AG + 5, g_half(1, 0), g_half(3, 0), y_dev),
        rc(AG + 6, g_half(2, 1), g_half(3, 1), x_dev),
        rc(AG + 7, gbuf.at[1, 0], gbuf.at[1, 1], c_dev),
        rc(AG + 8, gbuf.at[2, 0], gbuf.at[2, 1], c_dev),
        rc(AG + 9, gbuf.at[3, 0], gbuf.at[3, 1], c_dev),
    ]

    def term(d, dc):
        dy, dx = d // 2, d % 2
        yy, xx = y + dy - 2 * dy * y, x + dx - 2 * dx * x
        j = (yy * 2 + xx) * 2 + (c if dc == 0 else 1 - c)
        return dot3((rih[j], ril[j]), split(gbuf[d, dc]))

    for n in (0, 1, 4, 2, 3):
        ag[n].start()
    root_out[...] = term(0, 0)
    ag[0].wait_recv()
    ag[5].start()
    ag[1].wait_recv()
    ag[6].start()
    ag[4].wait_recv()
    root_out[...] += term(0, 1)
    ag[3].wait_recv()
    ag[7].start()
    ag[2].wait_recv()
    ag[8].start()
    root_out[...] += term(1, 0) + term(2, 0)
    ag[7].wait_recv()
    ag[8].wait_recv()
    root_out[...] += term(1, 1) + term(2, 1)
    ag[5].wait_recv()
    ag[6].wait_recv()
    ag[9].start()
    root_out[...] += term(3, 0)
    ag[9].wait_recv()
    root_out[...] += term(3, 1)
    for copy in ag:
        copy.wait_send()


def fused(low_rhs, low_inverse, panels, row_blocks, root_rhs, root_inverse):
    width, cols = low_rhs.shape
    own_rows, root = root_inverse.shape
    k_blocks = row_blocks.shape[1]
    blk = width // k_blocks
    vm = pltpu.VMEM
    any_spec = pl.BlockSpec(memory_space=pl.ANY)
    vm_spec = pl.BlockSpec(memory_space=vm)
    block = (own_rows, cols)
    return pl.pallas_call(
        kernel,
        out_shape=(jax.ShapeDtypeStruct(low_rhs.shape, F32), jax.ShapeDtypeStruct(root_rhs.shape, F32)),
        in_specs=[pl.BlockSpec(memory_space=pltpu.SMEM), any_spec, any_spec, any_spec, vm_spec, any_spec],
        out_specs=(any_spec, vm_spec),
        scratch_shapes=[
            vm((width, width), F32),
            vm((width, width), F32),
            vm((2, width, cols), F32),
            vm((2, width, cols), F32),
            vm((width, 2 * cols), BF16),
            vm((width, 2 * cols), BF16),
            vm((2 * (k_blocks + 1), blk, cols), F32),
            vm((4, 2) + block, F32),
            vm((4, 2) + block, F32),
            vm((4, 2) + block, F32),
            vm((2, 4, blk, cols), F32),
            vm((2, 2, blk, cols), F32),
            vm(block, F32),
            vm(block, F32),
            vm((4, 2) + block, F32),
            vm((own_rows, root), F32),
            vm((root // own_rows, own_rows, own_rows), BF16),
            vm((root // own_rows, own_rows, own_rows), BF16),
            pltpu.SemaphoreType.DMA((COPIES,)),
            pltpu.SemaphoreType.DMA((COPIES,)),
            pltpu.SemaphoreType.DMA((5,)),
        ],
        compiler_params=pltpu.CompilerParams(
            collective_id=0, has_side_effects=True, vmem_limit_bytes=56 * 2**20),
        cost_estimate=pl.CostEstimate(flops=2 * 10**10, bytes_accessed=10**7, transcendentals=0),
    )(row_blocks, low_rhs, low_inverse, panels, root_rhs, root_inverse)


def general(low_rhs, low_inverse, panels, row_blocks, root_rhs, root_inverse):
    cols = low_rhs.shape[1]
    k_blocks = row_blocks.shape[1]
    root = root_inverse.shape[1]
    blk = low_rhs.shape[0] // k_blocks
    high = lax.Precision.HIGHEST
    low_solution = jnp.dot(lax.all_gather(low_inverse, "grp", axis=0, tiled=True), low_rhs, precision=high)
    update = jnp.dot(lax.all_gather(panels, "grp", axis=0, tiled=True), low_solution, precision=high)
    onehot = (row_blocks[0][None, :] == jnp.arange(root // blk, dtype=jnp.int32)[:, None]).astype(F32)
    placed = jnp.dot(onehot, update.reshape(k_blocks, blk * cols), precision=high).reshape(root, cols)
    arrived = lax.all_to_all(placed, "leaf", split_axis=0, concat_axis=0, tiled=True)
    gathered = jnp.sum(arrived.reshape((-1,) + root_rhs.shape), axis=0)
    combined = lax.all_gather(root_rhs - gathered, "leaf", axis=0, tiled=True)
    return low_solution, jnp.dot(root_inverse, combined, precision=high)


def solution(mesh):
    placed = (
        P("leaf", "grp"),
        P(("leaf", "grp"), None),
        P(("leaf", "grp"), None),
        P("leaf", None),
        P("leaf", "grp"),
        P("leaf", None),
    )
    body = fused if (mesh.shape["leaf"], mesh.shape["grp"]) == (8, 4) else general
    return jax.shard_map(
        body,
        mesh=mesh,
        in_specs=placed,
        out_specs=(P("leaf", "grp"), P("leaf", "grp")),
        check_vma=False,
    )
```

```python
import functools

import jax
import jax.numpy as jnp
from jax import lax
from jax.experimental import pallas as pl
from jax.experimental.pallas import tpu as pltpu
from jax.sharding import PartitionSpec as P

MESH = pl.DeviceIdType.MESH
F32, BF16 = jnp.float32, jnp.bfloat16

LO, RO, PO = 0, 5, 9
LI, LF, PI, PF = 13, 18, 23, 27
XO, FO = 31, 35
CS, RA, RB, AG, RH = 37, 45, 53, 57, 67
COPIES = 68


def split(v):
    hi = v.astype(BF16)
    return hi, (v - hi.astype(F32)).astype(BF16)


def dot3(a, b):
    ah, al = a
    bh, bl = b
    d = functools.partial(jnp.dot, preferred_element_type=F32)
    return d(ah, bh) + (d(ah, bl) + d(al, bh))


def kernel(names, low_rhs, low_inverse, panels, root_rhs, root_inverse,
           low_out, root_out,
           lbuf, pbuf, rbuf, xbuf, xh, xl, vbuf, cbuf, tbuf, ra, rb, fs, rz,
           rib, lh, ll, ss, rs, ls):
    leaf, grp = lax.axis_index("leaf"), lax.axis_index("grp")
    planes = lax.axis_size("grp")
    width, cols = low_rhs.shape
    q_rows = low_inverse.shape[0]
    own_rows = root_rhs.shape[0]
    blk = own_rows // 2
    pc = q_rows // 4
    y, x, c = leaf // 4, (leaf // 2) % 2, leaf % 2
    inner = jnp.logical_and(grp > 0, grp < planes - 1)
    outer = jnp.logical_not(inner)
    low_side = grp < 2
    mate = jnp.where(low_side, 1 - grp, 5 - grp)
    other = 3 - grp
    side_q = jnp.where(low_side, 0, planes - 1)
    z_mate, z_other = (leaf, mate), (leaf, other)
    x_dev = (leaf + 2 - 4 * x, grp)
    y_dev = (leaf + 4 - 8 * y, grp)
    c_dev = (leaf + 1 - 2 * c, grp)

    def rc(n, src, dst, dev):
        return pltpu.make_async_remote_copy(
            src_ref=src, dst_ref=dst, send_sem=ss.at[n], recv_sem=rs.at[n],
            device_id=dev, device_id_type=MESH)

    def rows(start, n):
        return pl.ds(pl.multiple_of(start, n), n)

    edge = q_rows // 2

    def l_part(q, k):
        if k < 3:
            return 0, q_rows, pl.ds(k * q_rows, q_rows)
        if k == 3:
            return 0, q_rows, pl.ds(pl.multiple_of(q * q_rows, q_rows), edge)
        return edge, edge, pl.ds(pl.multiple_of(q * q_rows + edge, edge), edge)

    def l_need(k):
        return k + 1 if k < 3 else 0

    def l_slot(q, k):
        first, count, at = l_part(q, k)
        return lbuf.at[rows(q * q_rows + first, count), at]

    def p_slot(q, k):
        return pbuf.at[rows(q * q_rows + k * pc, pc)]

    def l_in(q, k):
        first, count, at = l_part(q, k)
        return low_inverse.at[pl.ds(first, count), at]

    def when(cond):
        return pl.when(cond)

    barrier = pltpu.get_barrier_semaphore()
    for dev in (x_dev, y_dev, c_dev, z_mate):
        pl.semaphore_signal(barrier, inc=1, device_id=dev, device_id_type=MESH)

    @when(inner)
    def _():
        pl.semaphore_signal(barrier, inc=1, device_id=z_other, device_id_type=MESH)

    n_root = root_inverse.shape[1] // blk
    ri_own = [pltpu.make_async_copy(root_inverse.at[:, pl.ds(k * blk, blk)], rib.at[0, 0, k], ls.at[5 + k])
              for k in range(n_root)]
    x_own = pltpu.make_async_copy(xbuf.at[1], low_out, ls.at[4])
    l_own = pltpu.make_async_copy(low_inverse, lbuf.at[rows(grp * q_rows, q_rows)], ls.at[1])
    p_own = pltpu.make_async_copy(panels, pbuf.at[rows(grp * q_rows, q_rows)], ls.at[2])
    r_own = pltpu.make_async_copy(low_rhs, rbuf.at[1], ls.at[3])

    @when(inner)
    def _():
        for copy in ri_own:
            copy.start()
        l_own.start()
        r_own.start()
        p_own.start()
        pl.semaphore_wait(barrier, 5)

    @when(outer)
    def _():
        pl.semaphore_wait(barrier, 4)

    quarter = width // 4

    def lo(k):
        return rc(LO + k, l_in(side_q, k), l_slot(side_q, k), z_mate)

    def ro(k):
        part = pl.ds(k * quarter, quarter)
        return rc(RO + k, low_rhs.at[part], rbuf.at[0, part], z_mate)

    def po(k):
        return rc(PO + k, panels.at[pl.ds(k * pc, pc)], p_slot(side_q, k), z_mate)

    def xo(k):
        part = pl.ds(k * quarter, quarter)
        return rc(XO + k, xbuf.at[0, part], low_out.at[part], z_mate)

    half = [pl.ds(0, blk), pl.ds(blk, blk)]
    f_out = [rc(FO + k, fs.at[half[k]], rz.at[half[k]], z_mate) for k in range(2)]

    rhs_in = rc(RH, root_rhs, rz, z_mate)

    @when(outer)
    def _():
        todo = [(l_need(k), lo(k)) for k in range(5)]
        todo += [(0, ro(k)) for k in range(4)] + [(0, po(k)) for k in range(4)]
        for n, (need, copy) in enumerate(todo):
            if n >= 3:
                before, earlier = todo[n - 3]

                @when(before <= grp)
                def _():
                    earlier.wait_send()

            @when(need <= grp)
            def _():
                copy.start()
        rhs_in.start()
        for need, copy in todo[-3:]:
            copy.wait_send()
        for k in range(4):
            xo(k).wait_recv()
        for k in range(2):
            f_out[k].wait_recv()
            root_out[half[k], :] = rz[half[k], :]
        rhs_in.wait_send()

    @when(inner)
    def _():
        def li(k, q):
            return rc(LI + k, l_in(grp, k), l_slot(q, k), z_other)

        def lf(k, q):
            return rc(LF + k, l_slot(q, k), l_slot(q, k), z_other)

        def pi(k, q):
            return rc(PI + k, panels.at[pl.ds(k * pc, pc)], p_slot(q, k), z_other)

        def pf(k, q):
            return rc(PF + k, p_slot(q, k), p_slot(q, k), z_other)

        far = planes - 1 - side_q
        for k in range(5):
            @when(l_need(k) <= grp)
            def _():
                li(k, grp).start()
        pi(0, grp).start()

        part_of = [pl.ds(0, n_root // 2), pl.ds(n_root // 2, n_root // 2)]

        def g_half(d, h):
            return rib.at[d, 0, part_of[h]]

        ag = [
            rc(AG, g_half(0, 0), g_half(1, 0), x_dev),
            rc(AG + 1, g_half(0, 1), g_half(2, 1), y_dev),
            rc(AG + 2, g_half(0, 0), g_half(2, 0), y_dev),
            rc(AG + 3, g_half(0, 1), g_half(1, 1), x_dev),
            rc(AG + 4, rib.at[0, 0], rib.at[0, 1], c_dev),
            rc(AG + 5, g_half(1, 0), g_half(3, 0), y_dev),
            rc(AG + 6, g_half(2, 1), g_half(3, 1), x_dev),
            rc(AG + 7, rib.at[1, 0], rib.at[1, 1], c_dev),
            rc(AG + 8, rib.at[2, 0], rib.at[2, 1], c_dev),
            rc(AG + 9, rib.at[3, 0], rib.at[3, 1], c_dev),
        ]
        for copy in ri_own:
            copy.wait()
        for n in (0, 1, 4):
            ag[n].start()
        for q in (side_q, other, far):
            lbuf[rows(q * q_rows, edge), pl.ds(pl.multiple_of(q * q_rows + edge, edge), edge)] = (
                jnp.zeros((edge, edge), F32))
        pi(1, grp).start()
        for k in range(5):
            @when(l_need(k) <= side_q)
            def _():
                lo(k).wait_recv()
                lf(k, side_q).start()
        for k in range(5):
            @when(l_need(k) <= grp)
            def _():
                li(k, grp).wait_send()
        for k in range(2, 4):
            pi(k, grp).start()

        for n in range(2):
            ag[n].wait_send()
            ag[3 - n if n == 0 else 2].start()
        for n in range(2):
            ag[n].wait_recv()
            ag[5 + n].start()

        l_own.wait()
        r_own.wait()
        for k in range(4):
            ro(k).wait_recv()
        for k in range(5):
            @when(l_need(k) <= other)
            def _():
                li(k, other).wait_recv()

            @when(l_need(k) <= far)
            def _():
                lf(k, far).wait_recv()
        for h in range(2):
            r_all = split(rbuf[h])
            for r in range(4):
                depth = (r + 1) * quarter
                here = slice(r * quarter, (r + 1) * quarter)
                part = dot3(split(lbuf[here, :depth]), (r_all[0][:depth], r_all[1][:depth]))
                xbuf[h, here] = part
                hi, lo_part = split(part)
                xh[here, h * cols:(h + 1) * cols] = hi
                xl[here, h * cols:(h + 1) * cols] = lo_part
                if h == 0:
                    xo(r).start()
        x_own.start()

        per = q_rows // blk

        def update(first, count, h):
            at = slice(h * cols, (h + 1) * cols)
            panel = split(pbuf[rows(first * blk, count * blk), :])
            return dot3(panel, (xh[:, at], xl[:, at]))

        def columns(r0, r1):
            for d in range(4):
                for dc in range(2):
                    both = jnp.concatenate([rib[d, dc, r0], rib[d, dc, r1]], axis=1)
                    hi, lo_part = split(both)
                    lh[d, dc] = hi
                    ll[d, dc] = lo_part

        def named(q):
            columns(names[0, q * per], names[0, q * per + 1])

        def place(h, value, first=False):
            val = split(value)
            for d in range(4):
                for dc in range(2):
                    term = dot3((lh[d, dc], ll[d, dc]), val)
                    vbuf[d, dc, h] = term if first else vbuf[d, dc, h] - term

        order = (3, 1, 2, 0)
        top, low = half
        cs, steps, b0, b1 = [], [], [], []
        for h in range(2):
            cs.append([rc(CS + 4 * h + d, vbuf.at[d, 1, h], cbuf.at[d, h], c_dev) for d in range(4)])
            steps.append([
                rc(RA + 4 * h, tbuf.at[1, h, top], ra.at[h, 0], x_dev),
                rc(RA + 4 * h + 1, tbuf.at[3, h, top], ra.at[h, 1], x_dev),
                rc(RA + 4 * h + 2, tbuf.at[2, h, low], ra.at[h, 2], y_dev),
                rc(RA + 4 * h + 3, tbuf.at[3, h, low], ra.at[h, 3], y_dev)])
            b0.append(rc(RB + 2 * h, tbuf.at[2, h, top], rb.at[h, 0], y_dev))
            b1.append(rc(RB + 2 * h + 1, tbuf.at[1, h, low], rb.at[h, 1], x_dev))

        def to_core(h):
            for d in order:
                cs[h][d].start()

        def from_core(h):
            for d in order:
                cs[h][d].wait_recv()
                tbuf[d, h] = vbuf[d, 0, h] + cbuf[d, h]
                for n in {3: (1, 3), 1: (0,), 2: (2,), 0: ()}[d]:
                    steps[h][n].start()

        def second(h):
            steps[h][1].wait_recv()
            tbuf[2, h, top] += ra[h, 1]
            b0[h].start()
            steps[h][3].wait_recv()
            tbuf[1, h, low] += ra[h, 3]
            b1[h].start()

        def final(h, k):
            steps[h][2 * k].wait_recv()
            (b0, b1)[k][h].wait_recv()
            return tbuf[0, h, half[k]] + ra[h, 2 * k] + rb[h, k]

        for k in range(4):
            po(k).wait_recv()
            pf(k, side_q).start()
        ag[2].wait_recv()
        ag[3].wait_recv()
        ag[7].start()
        ag[8].start()
        p_own.wait()
        rhs_in.wait_recv()
        for k in range(4):
            pi(k, other).wait_recv()
        ag[5].wait_recv()
        ag[6].wait_recv()
        ag[9].start()
        for n in (4, 7, 8, 9):
            ag[n].wait_recv()
        columns(2 * leaf, 2 * leaf + 1)
        place(0, rz[...], True)
        place(1, root_rhs[...], True)
        for q in (grp, side_q, other):
            named(q)
            for h in range(2):
                place(h, update(q * per, per, h))
        named(far)
        for k in range(4):
            pf(k, far).wait_recv()
        place(0, update(far * per, per, 0))
        to_core(0)
        place(1, update(far * per, per, 1))
        to_core(1)
        from_core(0)
        second(0)
        from_core(1)
        for k in range(2):
            fs[half[k], :] = final(0, k)
            f_out[k].start()
        second(1)
        for k in range(2):
            root_out[half[k], :] = final(1, k)
        for k in range(5):
            @when(l_need(k) <= side_q)
            def _():
                lf(k, side_q).wait_send()
        for k in range(4):
            pi(k, grp).wait_send()
            pf(k, side_q).wait_send()
            xo(k).wait_send()
        for copy in cs[0] + cs[1] + steps[0] + steps[1] + b0 + b1 + f_out + ag[2:]:
            copy.wait_send()
        x_own.wait()


def fused(low_rhs, low_inverse, panels, row_blocks, root_rhs, root_inverse):
    width, cols = low_rhs.shape
    own_rows, root = root_inverse.shape
    k_blocks = row_blocks.shape[1]
    blk = width // k_blocks
    vm = pltpu.VMEM
    any_spec = pl.BlockSpec(memory_space=pl.ANY)
    vm_spec = pl.BlockSpec(memory_space=vm)
    block = (own_rows, cols)
    return pl.pallas_call(
        kernel,
        out_shape=(jax.ShapeDtypeStruct(low_rhs.shape, F32), jax.ShapeDtypeStruct(root_rhs.shape, F32)),
        in_specs=[pl.BlockSpec(memory_space=pltpu.SMEM), any_spec, any_spec, any_spec, vm_spec, any_spec],
        out_specs=(any_spec, vm_spec),
        scratch_shapes=[
            vm((width, width), F32),
            vm((width, width), F32),
            vm((2, width, cols), F32),
            vm((2, width, cols), F32),
            vm((width, 2 * cols), BF16),
            vm((width, 2 * cols), BF16),
            vm((4, 2, 2) + block, F32),
            vm((4, 2) + block, F32),
            vm((4, 2) + block, F32),
            vm((2, 4, blk, cols), F32),
            vm((2, 2, blk, cols), F32),
            vm(block, F32),
            vm(block, F32),
            vm((4, 2, root // blk, own_rows, blk), F32),
            vm((4, 2, own_rows, own_rows), BF16),
            vm((4, 2, own_rows, own_rows), BF16),
            pltpu.SemaphoreType.DMA((COPIES,)),
            pltpu.SemaphoreType.DMA((COPIES,)),
            pltpu.SemaphoreType.DMA((5 + root // blk,)),
        ],
        compiler_params=pltpu.CompilerParams(
            collective_id=0, has_side_effects=True, vmem_limit_bytes=56 * 2**20),
        cost_estimate=pl.CostEstimate(flops=2 * 10**10, bytes_accessed=10**7, transcendentals=0),
    )(row_blocks, low_rhs, low_inverse, panels, root_rhs, root_inverse)


def general(low_rhs, low_inverse, panels, row_blocks, root_rhs, root_inverse):
    cols = low_rhs.shape[1]
    k_blocks = row_blocks.shape[1]
    root = root_inverse.shape[1]
    blk = low_rhs.shape[0] // k_blocks
    high = lax.Precision.HIGHEST
    low_solution = jnp.dot(lax.all_gather(low_inverse, "grp", axis=0, tiled=True), low_rhs, precision=high)
    update = jnp.dot(lax.all_gather(panels, "grp", axis=0, tiled=True), low_solution, precision=high)
    onehot = (row_blocks[0][None, :] == jnp.arange(root // blk, dtype=jnp.int32)[:, None]).astype(F32)
    placed = jnp.dot(onehot, update.reshape(k_blocks, blk * cols), precision=high).reshape(root, cols)
    arrived = lax.all_to_all(placed, "leaf", split_axis=0, concat_axis=0, tiled=True)
    gathered = jnp.sum(arrived.reshape((-1,) + root_rhs.shape), axis=0)
    combined = lax.all_gather(root_rhs - gathered, "leaf", axis=0, tiled=True)
    return low_solution, jnp.dot(root_inverse, combined, precision=high)


def solution(mesh):
    placed = (
        P("leaf", "grp"),
        P(("leaf", "grp"), None),
        P(("leaf", "grp"), None),
        P("leaf", None),
        P("leaf", "grp"),
        P("leaf", None),
    )
    body = fused if (mesh.shape["leaf"], mesh.shape["grp"]) == (8, 4) else general
    return jax.shard_map(
        body,
        mesh=mesh,
        in_specs=placed,
        out_specs=(P("leaf", "grp"), P("leaf", "grp")),
        check_vma=False,
    )
```
